256 devices in a mesh: seq: 32 (over z, y_lo, core), dp: 8 (over x, y_hi).
Axes of the slice: x: 4, y: 4 (y_hi: 2, y_lo: 2; y = y_hi * 2 + y_lo), z: 8, core: 2. Of those that a mesh axis runs over, the one named last changes fastest.
Arguments:
- enc_query: bfloat16 [32768, 4096], P(('dp', 'seq')), parts along dimension 0, may hold values from -6 to 6
- enc_key: bfloat16 [32768, 4096], P(('dp', 'seq')), parts along dimension 0, may hold values from -6 to 6
- enc_value: bfloat16 [32768, 4096], P(('dp', 'seq')), parts along dimension 0, may hold values from -6 to 6
- dec_query: bfloat16 [8192, 4096], P(('dp', 'seq')), parts along dimension 0, may hold values from -6 to 6
- enc_length: int32 [8], P('dp'), parts along dimension 0, may hold values from 2048 to 4096
- tgt_length: int32 [8], P('dp'), parts along dimension 0, may hold values from 512 to 1024
Outputs:
- enc_mixed: bfloat16 [32768, 4096], P(('dp', 'seq')), parts along dimension 0
- cross_mixed: bfloat16 [8192, 4096], P(('dp', 'seq')), parts along dimension 0
The draws below stay inside these ranges and needn't reach their ends.
There are 8 independent parts, one for each index of `dp`. The reference program is written for one: setup_inputs(seed, part) draws one part's arguments, and reference() takes and returns one part's arrays. A program takes and returns all parts, laid end to end along the dimension named above; each array names one. Nothing has to cross between parts.
All inputs are finite; a program needn't handle non-finite values.
Results may differ from the reference program's by a relative error of at most 0.0049.
Values may be sent and summed in bfloat16 or wider, within the bound.
No kernel may reach another device: no remote copies, remote signals or barrier semaphores. Data moves between devices by JAX's collectives and lax.ppermute only.
A program may use at most 128 MiB of HBM per device.

```python
import jax
import jax.numpy as jnp
from jax import lax

H = 64
DH = 64
HD = 4096
LEN = 4096
TGT = 1024


def key_field(key):
    base_field = jnp.clip(jax.random.normal(key, (LEN, HD), jnp.float32), -4.0, 4.0)
    return base_field


def draw_enc_key(key, part):
    return key_field(key).astype(jnp.bfloat16)


def draw_enc_query(key, part):
    key = jax.random.fold_in(key, 11)
    drawn = jnp.clip(jax.random.normal(key, (LEN, HD), jnp.float32), -6.0, 6.0)
    return drawn.astype(jnp.bfloat16)


def draw_dec_query(key, part):
    key = jax.random.fold_in(key, 12)
    drawn = jnp.clip(jax.random.normal(key, (TGT, HD), jnp.float32), -6.0, 6.0)
    return drawn.astype(jnp.bfloat16)


def block_levels(own_key, shape, pieces, low, largest):
    def one(position, parts):
        draws = jax.random.uniform(jax.random.fold_in(jax.random.fold_in(own_key, 6), position), (parts,), jnp.float32, low / len(pieces), largest / len(pieces))
        return jnp.repeat(jnp.exp(draws), shape[position] // parts).reshape((-1,) + (1,) * (len(shape) - position - 1))

    level = one(*pieces[0])
    for cut in pieces[1:]:
        level = level * one(*cut)
    return level


def noise(own_key, shape, deviation, reach, shards=(), kind=jnp.bfloat16):
    drawn = deviation * jax.random.normal(own_key, shape, jnp.float32)
    if shards:
        drawn = drawn * block_levels(own_key, shape, shards, -0.22, 0.18)
    return jnp.clip(drawn, -reach, reach).astype(kind)


def setup_inputs(seed: int = 0, part: int = 0) -> dict:
    key_list = jax.random.split(jax.random.key(seed), 7)
    part_splits = jax.random.split(jax.random.fold_in(key_list[6], part), 7)
    return {
        "enc_query": draw_enc_query(jax.random.fold_in(jax.random.fold_in(key_list[6], part), 71), part),
        "enc_key": draw_enc_key(jax.random.fold_in(jax.random.fold_in(key_list[6], part), 71), part),
        "enc_value": noise(part_splits[2], (LEN, HD), 1.0, 6.0, ((0, 32),)),
        "dec_query": draw_dec_query(jax.random.fold_in(jax.random.fold_in(key_list[6], part), 71), part),
        "enc_length": jax.random.randint(part_splits[4], (1,), LEN // 2, LEN + 1).astype(jnp.int32),
        "tgt_length": jax.random.randint(part_splits[5], (1,), TGT // 2, TGT + 1).astype(jnp.int32),
    }


score_scale = 0.125


def attend(queries, key_mat, values, valid_len):
    scores = jnp.dot(queries, key_mat.T, preferred_element_type=jnp.float32) * score_scale
    live_keys = jnp.arange(key_mat.shape[0], dtype=jnp.int32) < valid_len
    scores = jnp.where(live_keys[None, :], scores, -1e30)
    row_max = jnp.max(scores, axis=-1, keepdims=True)
    weights = jnp.exp(scores - row_max)
    weights = (weights / jnp.sum(weights, axis=-1, keepdims=True)).astype(jnp.bfloat16)
    return jnp.dot(weights, values, preferred_element_type=jnp.float32).astype(jnp.bfloat16)


def split_heads(matrix):
    return matrix.reshape(matrix.shape[0], H, DH).transpose(1, 0, 2)


def all_heads(queries, key_mat, values, valid_len):
    row_total = queries.shape[0]
    stacked = (split_heads(queries), split_heads(key_mat), split_heads(values))
    result = lax.map(lambda triple: attend(triple[0], triple[1], triple[2], valid_len), stacked)
    return result.transpose(1, 0, 2).reshape(row_total, H * DH)


def reference(enc_query, enc_key, enc_value, dec_query, enc_length, tgt_length):
    enc_mixed = all_heads(enc_query, enc_key, enc_value, enc_length[0])
    crossed = all_heads(dec_query, enc_key, enc_value, enc_length[0])
    keep_rows = jnp.arange(TGT, dtype=jnp.int32) < tgt_length[0]
    cross_mixed = jnp.where(keep_rows[:, None], crossed, jnp.zeros_like(crossed))
    return enc_mixed, cross_mixed
```

```python
import math

import jax
import jax.numpy as jnp
from jax import lax
from jax.experimental import pallas as pl
from jax.experimental.pallas import tpu as pltpu
from jax.sharding import PartitionSpec as P

DH = 64
LANES = 128
SCALE = 0.125
EXP2_SCALE = SCALE * math.log2(math.e)
SUM_LOW, SUM_HIGH = 2.0**-60, 2.0**100
QUERY_BLOCK = 512
KEY_BLOCK = 4096
SLOW_KEYS = 512
VMEM_BYTES = 56 << 20
CONTRACT_LAST = (((1,), (1,)), ((), ()))


def prepare_kernel(length_ref, kv_ref, key_ref, value_ref):
    length = length_ref[0]
    sources = kv_ref.shape[0]
    rows = kv_ref.shape[1] // 2
    group = max(1, 512 // rows)

    def step(g, carry):
        keys = kv_ref[pl.ds(g * group, group), :rows, :].reshape(group * rows, LANES)
        values = kv_ref[pl.ds(g * group, group), rows:, :].reshape(group * rows, LANES)
        start = pl.multiple_of(g * group * rows, group * rows)
        position = start + lax.broadcasted_iota(jnp.int32, (group * rows, LANES), 0)
        live = position < length
        first_key = kv_ref[0, 0:1, :]
        key_ref[pl.ds(start, group * rows), :] = jnp.where(live, keys, first_key)
        flipped = jnp.where(live, values, jnp.zeros_like(values)).astype(jnp.float32).T
        flipped = flipped.astype(jnp.bfloat16)
        along = start + lax.broadcasted_iota(jnp.int32, (16, group * rows), 1)
        ones = jnp.where(along < length, 1.0, 0.0).astype(jnp.bfloat16)
        for head in range(2):
            value_ref[head, :DH, pl.ds(start, group * rows)] = flipped[head * DH : (head + 1) * DH]
            value_ref[head, DH:, pl.ds(start, group * rows)] = ones
        return carry

    lax.fori_loop(0, sources // group, step, 0)


def prepare(valid_len, kv):
    keys = kv.shape[0] * kv.shape[1] // 2
    vmem = pl.BlockSpec(memory_space=pltpu.VMEM)
    return pl.pallas_call(
        prepare_kernel,
        in_specs=[pl.BlockSpec(memory_space=pltpu.SMEM), vmem],
        out_specs=[vmem, vmem],
        out_shape=[
            jax.ShapeDtypeStruct((keys, LANES), jnp.bfloat16),
            jax.ShapeDtypeStruct((2, DH + 16, keys), jnp.bfloat16),
        ],
        compiler_params=pltpu.CompilerParams(vmem_limit_bytes=VMEM_BYTES),
        cost_estimate=pl.CostEstimate(flops=0, bytes_accessed=6 << 20, transcendentals=0),
    )(valid_len, kv)


def attend_kernel(query_ref, key_ref, value_ref, out_ref, score_ref):
    keys = key_ref.shape[0]
    lane = lax.broadcasted_iota(jnp.int32, (QUERY_BLOCK, LANES), 1)

    def head_queries(queries):
        zeros = jnp.zeros_like(queries)
        return [jnp.where(lane < DH, queries, zeros), jnp.where(lane < DH, zeros, queries)]

    def scores(queries, start, count):
        return lax.dot_general(
            key_ref[pl.ds(start, count), :], queries, CONTRACT_LAST, preferred_element_type=jnp.float32
        )

    def weigh(head, weights, start, count):
        return jnp.dot(
            value_ref[head, :, pl.ds(start, count)],
            weights.astype(jnp.bfloat16),
            preferred_element_type=jnp.float32,
        )

    def store(rows, totals):
        mixed = jnp.concatenate([t[:DH] / t[DH : DH + 1] for t in totals], axis=0)
        out_ref[rows, :] = mixed.T.astype(jnp.bfloat16)

    def block(index, carry):
        rows = pl.ds(pl.multiple_of(index * QUERY_BLOCK, QUERY_BLOCK), QUERY_BLOCK)
        queries = head_queries(query_ref[rows, :])
        totals = []
        for head in range(2):
            total = None
            for start in range(0, keys, KEY_BLOCK):
                weights = jnp.exp2(scores(queries[head], start, KEY_BLOCK) * EXP2_SCALE)
                part = weigh(head, weights, start, KEY_BLOCK)
                total = part if total is None else total + part
            totals.append(total)
        store(rows, totals)
        sums = jnp.concatenate([t[DH : DH + 8] for t in totals], axis=0)
        safe = jnp.logical_and(sums >= SUM_LOW, sums <= SUM_HIGH)
        unsafe = jnp.max(jnp.where(safe, 0.0, 1.0)) > 0.0

        @pl.when(unsafe)
        def _():
            totals = []
            for head in range(2):

                def first(i, top):
                    start = pl.multiple_of(i * SLOW_KEYS, SLOW_KEYS)
                    found = scores(queries[head], start, SLOW_KEYS)
                    score_ref[pl.ds(start, SLOW_KEYS), :] = found
                    return jnp.maximum(top, jnp.max(found, axis=0, keepdims=True))

                top = lax.fori_loop(
                    0, keys // SLOW_KEYS, first, jnp.full((1, QUERY_BLOCK), -jnp.inf, jnp.float32)
                )

                def second(i, total):
                    start = pl.multiple_of(i * SLOW_KEYS, SLOW_KEYS)
                    found = score_ref[pl.ds(start, SLOW_KEYS), :]
                    return total + weigh(head, jnp.exp2((found - top) * EXP2_SCALE), start, SLOW_KEYS)

                totals.append(
                    lax.fori_loop(
                        0, keys // SLOW_KEYS, second, jnp.zeros((DH + 16, QUERY_BLOCK), jnp.float32)
                    )
                )
            store(rows, totals)

        return carry

    lax.fori_loop(0, query_ref.shape[0] // QUERY_BLOCK, block, 0)


def attend(queries, keys, values):
    sources, rows, _ = queries.shape
    total, count = sources * rows, keys.shape[0]
    vmem = pl.BlockSpec(memory_space=pltpu.VMEM)
    result = pl.pallas_call(
        attend_kernel,
        in_specs=[vmem, vmem, vmem],
        out_specs=vmem,
        out_shape=jax.ShapeDtypeStruct((total, LANES), jnp.bfloat16),
        scratch_shapes=[pltpu.VMEM((count, QUERY_BLOCK), jnp.float32)],
        compiler_params=pltpu.CompilerParams(vmem_limit_bytes=VMEM_BYTES),
        cost_estimate=pl.CostEstimate(
            flops=total * count * 2 * 512 * 2, bytes_accessed=4 << 20, transcendentals=total * count * 2
        ),
    )(queries.reshape(total, LANES), keys, values)
    return result.reshape(sources, rows, LANES)


def by_owner(rows):
    return rows.reshape(rows.shape[0], -1, LANES).transpose(1, 0, 2)


def by_row(blocks):
    return blocks.transpose(1, 0, 2).reshape(blocks.shape[1], -1)


def exchange(blocks):
    return lax.all_to_all(blocks, "seq", split_axis=0, concat_axis=0, tiled=True)


def on_device(enc_query, enc_key, enc_value, dec_query, enc_length, tgt_length):
    rows_local = dec_query.shape[0]
    kv = exchange(by_owner(jnp.concatenate([enc_key, enc_value], axis=0)))
    cuts = (0, 32, 96, 128)
    sent = [by_owner(enc_query[a:b]) for a, b in zip(cuts, cuts[1:])]
    sent[0] = jnp.concatenate([by_owner(dec_query), sent[0]], axis=1)
    arrived = [exchange(s) for s in sent]
    keys, values = prepare(enc_length, kv)
    returned = [exchange(attend(q, keys, values)) for q in arrived]
    returned_cross, returned[0] = returned[0][:, :rows_local], returned[0][:, rows_local:]
    enc_mixed = jnp.concatenate([by_row(r) for r in returned], axis=0)
    first_row = lax.axis_index("seq") * rows_local
    keep_rows = first_row + jnp.arange(rows_local, dtype=jnp.int32) < tgt_length[0]
    crossed = by_row(returned_cross)
    cross_mixed = jnp.where(keep_rows[:, None], crossed, jnp.zeros_like(crossed))
    return (enc_mixed, cross_mixed)


def solution(mesh):
    return jax.shard_map(
        on_device,
        mesh=mesh,
        in_specs=(
            P(("dp", "seq"), None),
            P(("dp", "seq"), None),
            P(("dp", "seq"), None),
            P(("dp", "seq"), None),
            P("dp"),
            P("dp"),
        ),
        out_specs=(P(("dp", "seq"), None), P(("dp", "seq"), None)),
        check_vma=False,
    )
```

```python
import functools
import math

import jax
import jax.numpy as jnp
from jax import lax
from jax.experimental import pallas as pl
from jax.experimental.pallas import tpu as pltpu
from jax.sharding import PartitionSpec as P

DH = 64
LANES = 128
SCALE = 0.125
EXP2_SCALE = SCALE * math.log2(math.e)
SUM_LOW, SUM_HIGH = 2.0**-60, 2.0**100
SOURCES_AT_ONCE = 8
KEY_BLOCK = 4096
SLOW_KEYS = 512
VMEM_BYTES = 56 << 20
CONTRACT_LAST = (((1,), (1,)), ((), ()))


def prepare_kernel(rows, length_ref, kv_ref, key_ref, value_ref):
    length = length_ref[0]
    sources = kv_ref.shape[0]
    group = max(1, 512 // rows)

    def step(g, carry):
        keys = kv_ref[pl.ds(g * group, group), :rows, :].reshape(group * rows, LANES)
        values = kv_ref[pl.ds(g * group, group), rows : 2 * rows, :].reshape(group * rows, LANES)
        start = pl.multiple_of(g * group * rows, group * rows)
        position = start + lax.broadcasted_iota(jnp.int32, (group * rows, LANES), 0)
        live = position < length
        first_key = kv_ref[0, 0:1, :]
        key_ref[pl.ds(start, group * rows), :] = jnp.where(live, keys, first_key)
        flipped = jnp.where(live, values, jnp.zeros_like(values)).astype(jnp.float32).T
        flipped = flipped.astype(jnp.bfloat16)
        along = start + lax.broadcasted_iota(jnp.int32, (16, group * rows), 1)
        ones = jnp.where(along < length, 1.0, 0.0).astype(jnp.bfloat16)
        for head in range(2):
            value_ref[head, :DH, pl.ds(start, group * rows)] = flipped[head * DH : (head + 1) * DH]
            value_ref[head, DH:, pl.ds(start, group * rows)] = ones
        return carry

    lax.fori_loop(0, sources // group, step, 0)


def prepare(valid_len, kv, rows):
    keys = kv.shape[0] * rows
    vmem = pl.BlockSpec(memory_space=pltpu.VMEM)
    return pl.pallas_call(
        functools.partial(prepare_kernel, rows),
        in_specs=[pl.BlockSpec(memory_space=pltpu.SMEM), vmem],
        out_specs=[vmem, vmem],
        out_shape=[
            jax.ShapeDtypeStruct((keys, LANES), jnp.bfloat16),
            jax.ShapeDtypeStruct((2, DH + 16, keys), jnp.bfloat16),
        ],
        compiler_params=pltpu.CompilerParams(vmem_limit_bytes=VMEM_BYTES),
        cost_estimate=pl.CostEstimate(flops=0, bytes_accessed=6 << 20, transcendentals=0),
    )(valid_len, kv)


def attend_kernel(begin, query_ref, key_ref, value_ref, out_ref, score_ref):
    keys = key_ref.shape[0]
    part = out_ref.shape[1]
    group = SOURCES_AT_ONCE
    block_rows = group * part
    lane = lax.broadcasted_iota(jnp.int32, (block_rows, LANES), 1)

    def head_queries(queries):
        zeros = jnp.zeros_like(queries)
        return [jnp.where(lane < DH, queries, zeros), jnp.where(lane < DH, zeros, queries)]

    def scores(queries, start, count):
        return lax.dot_general(
            key_ref[pl.ds(start, count), :], queries, CONTRACT_LAST, preferred_element_type=jnp.float32
        )

    def weigh(head, weights, start, count):
        return jnp.dot(
            value_ref[head, :, pl.ds(start, count)],
            weights.astype(jnp.bfloat16),
            preferred_element_type=jnp.float32,
        )

    def store(sources, totals):
        mixed = jnp.concatenate([t[:DH] / t[DH : DH + 1] for t in totals], axis=0)
        out_ref[sources] = mixed.T.astype(jnp.bfloat16).reshape(group, part, LANES)

    def block(index, carry):
        sources = pl.ds(index * group, group)
        block_queries = query_ref[sources, begin : begin + part, :]
        queries = head_queries(block_queries.reshape(block_rows, LANES))
        totals = []
        for head in range(2):
            total = None
            for start in range(0, keys, KEY_BLOCK):
                weights = jnp.exp2(scores(queries[head], start, KEY_BLOCK) * EXP2_SCALE)
                found = weigh(head, weights, start, KEY_BLOCK)
                total = found if total is None else total + found
            totals.append(total)
        store(sources, totals)
        sums = jnp.concatenate([t[DH : DH + 8] for t in totals], axis=0)
        safe = jnp.logical_and(sums >= SUM_LOW, sums <= SUM_HIGH)
        unsafe = jnp.max(jnp.where(safe, 0.0, 1.0)) > 0.0

        @pl.when(unsafe)
        def _():
            totals = []
            for head in range(2):

                def first(i, top):
                    start = pl.multiple_of(i * SLOW_KEYS, SLOW_KEYS)
                    found = scores(queries[head], start, SLOW_KEYS)
                    score_ref[pl.ds(start, SLOW_KEYS), :] = found
                    return jnp.maximum(top, jnp.max(found, axis=0, keepdims=True))

                top = lax.fori_loop(
                    0, keys // SLOW_KEYS, first, jnp.full((1, block_rows), -jnp.inf, jnp.float32)
                )

                def second(i, total):
                    start = pl.multiple_of(i * SLOW_KEYS, SLOW_KEYS)
                    found = score_ref[pl.ds(start, SLOW_KEYS), :]
                    return total + weigh(head, jnp.exp2((found - top) * EXP2_SCALE), start, SLOW_KEYS)

                totals.append(
                    lax.fori_loop(
                        0, keys // SLOW_KEYS, second, jnp.zeros((DH + 16, block_rows), jnp.float32)
                    )
                )
            store(sources, totals)

        return carry

    lax.fori_loop(0, out_ref.shape[0] // group, block, 0)


def attend(queries, begin, part, keys, values):
    sources, count = queries.shape[0], keys.shape[0]
    total = sources * part
    vmem = pl.BlockSpec(memory_space=pltpu.VMEM)
    return pl.pallas_call(
        functools.partial(attend_kernel, begin),
        in_specs=[vmem, vmem, vmem],
        out_specs=vmem,
        out_shape=jax.ShapeDtypeStruct((sources, part, LANES), jnp.bfloat16),
        scratch_shapes=[pltpu.VMEM((count, SOURCES_AT_ONCE * part), jnp.float32)],
        compiler_params=pltpu.CompilerParams(vmem_limit_bytes=VMEM_BYTES),
        cost_estimate=pl.CostEstimate(
            flops=total * count * 2 * 512 * 2, bytes_accessed=4 << 20, transcendentals=total * count * 2
        ),
    )(queries, keys, values)


def by_owner(rows):
    return rows.reshape(rows.shape[0], -1, LANES).transpose(1, 0, 2)


def by_row(blocks):
    return blocks.transpose(1, 0, 2).reshape(blocks.shape[1], -1)


def exchange(blocks):
    return lax.all_to_all(blocks, "seq", split_axis=0, concat_axis=0, tiled=True)


def on_device(enc_query, enc_key, enc_value, dec_query, enc_length, tgt_length):
    rows_local = dec_query.shape[0]
    rows = enc_key.shape[0]
    cut = 2 * rows_local
    first = exchange(by_owner(jnp.concatenate([enc_key, enc_value, dec_query, enc_query[:cut]], axis=0)))
    late, first = lax.optimization_barrier((by_owner(enc_query[cut:]), first))
    late = exchange(late)
    keys, values = prepare(enc_length, first, rows)
    mixed = attend(first, 2 * rows, rows_local + cut, keys, values)
    mixed, late = lax.optimization_barrier((mixed, late))
    returned = [exchange(mixed)]
    mixed = attend(late, 0, rows - cut, keys, values)
    mixed, returned[0] = lax.optimization_barrier((mixed, returned[0]))
    returned.append(exchange(mixed))
    returned_cross, returned[0] = returned[0][:, :rows_local], returned[0][:, rows_local:]
    enc_mixed = jnp.concatenate([by_row(r) for r in returned], axis=0)
    first_row = lax.axis_index("seq") * rows_local
    keep_rows = first_row + jnp.arange(rows_local, dtype=jnp.int32) < tgt_length[0]
    crossed = by_row(returned_cross)
    cross_mixed = jnp.where(keep_rows[:, None], crossed, jnp.zeros_like(crossed))
    return (enc_mixed, cross_mixed)


def solution(mesh):
    return jax.shard_map(
        on_device,
        mesh=mesh,
        in_specs=(
            P(("dp", "seq"), None),
            P(("dp", "seq"), None),
            P(("dp", "seq"), None),
            P(("dp", "seq"), None),
            P("dp"),
            P("dp"),
        ),
        out_specs=(P(("dp", "seq"), None), P(("dp", "seq"), None)),
        check_vma=False,
    )
```

```python
import functools
import math

import jax
import jax.numpy as jnp
from jax import lax
from jax.experimental import pallas as pl
from jax.experimental.pallas import tpu as pltpu
from jax.sharding import PartitionSpec as P

DH = 64
LANES = 128
SCALE = 0.125
EXP2_SCALE = SCALE * math.log2(math.e)
SUM_LOW, SUM_HIGH = 2.0**-60, 2.0**100
SOURCES_AT_ONCE = 8
SLOW_KEYS = 512
VMEM_BYTES = 56 << 20
SMEM = pl.BlockSpec(memory_space=pltpu.SMEM)
VMEM = pl.BlockSpec(memory_space=pltpu.VMEM)
HBM = pl.BlockSpec(memory_space=pl.ANY)
CONTRACT_FIRST = (((0,), (0,)), ((), ()))
CONTRACT_LAST = (((1,), (1,)), ((), ()))


def prepare(length, rows, offset, stride, block_ref, copies, key_ref, value_ref):
    group = block_ref.shape[0] // len(copies)
    count = group * rows
    for g, copy in enumerate(copies):
        copy.wait()
        sources = slice(g * group, (g + 1) * group)
        keys = block_ref[sources, :rows, :].reshape(count, LANES)
        values = block_ref[sources, rows : 2 * rows, :].reshape(count, LANES)

        def live(axis, shape):
            i = lax.broadcasted_iota(jnp.int32, shape, axis)
            return i + lax.div(i, rows) * (stride - rows) + (g * group * stride + offset) < length

        here = slice(g * count, (g + 1) * count)
        kept = live(0, (count, LANES))
        zeros = jnp.zeros_like(keys)
        key_ref[here, :] = jnp.where(kept, keys, zeros)
        flipped = jnp.where(kept, values, zeros).T
        ones = jnp.where(live(1, (16, count)), 1.0, 0.0).astype(jnp.bfloat16)
        for head in range(2):
            value_ref[head, :DH, here] = flipped[head * DH : (head + 1) * DH]
            value_ref[head, DH:, here] = ones


def at_once(rows):
    return 512 // rows if 512 % rows == 0 else 4


def arrive(source, block, sems, rows):
    group = at_once(rows)
    copies = []
    for g in range(block.shape[0] // group):
        here = pl.ds(g * group, group)
        copies.append(pltpu.make_async_copy(source.at[here], block.at[here], sems.at[g]))
        copies[-1].start()
    return copies


def scores(key_ref, queries, start, count):
    return lax.dot_general(
        key_ref[pl.ds(start, count), :], queries, CONTRACT_LAST, preferred_element_type=jnp.float32
    )


def weigh(value_ref, head, weights, start, count):
    return jnp.dot(
        value_ref[head, :, pl.ds(start, count)], weights.astype(jnp.bfloat16), preferred_element_type=jnp.float32
    )


def quick(head, queries, key_ref, value_ref):
    keys = key_ref.shape[0]
    weights = jnp.exp2(scores(key_ref, queries, 0, keys) * EXP2_SCALE)
    return weigh(value_ref, head, weights, 0, keys)


def head_queries(query_ref, sources, begin, part):
    block_rows = SOURCES_AT_ONCE * part
    queries = query_ref[sources, begin : begin + part, :].reshape(block_rows, LANES)
    lane = lax.broadcasted_iota(jnp.int32, (block_rows, LANES), 1)
    zeros = jnp.zeros_like(queries)
    return [jnp.where(lane < DH, queries, zeros), jnp.where(lane < DH, zeros, queries)]


def begin_rows(begin, part, query_ref, key_ref, value_ref, total_ref):
    def block(index, carry):
        queries = head_queries(query_ref, pl.ds(index * SOURCES_AT_ONCE, SOURCES_AT_ONCE), begin, part)
        for head in range(2):
            total_ref[index, head] = quick(head, queries[head], key_ref, value_ref)
        return carry

    lax.fori_loop(0, total_ref.shape[0], block, 0)


def finish_rows(begin, part, query_ref, parts, total_ref, out_ref, fetch_first=None):
    block_rows = SOURCES_AT_ONCE * part

    def block(index, carry):
        sources = pl.ds(index * SOURCES_AT_ONCE, SOURCES_AT_ONCE)
        queries = head_queries(query_ref, sources, begin, part)

        def store(totals):
            mixed = jnp.concatenate([t[:DH] / t[DH : DH + 1] for t in totals], axis=0)
            out_ref[sources] = mixed.T.astype(jnp.bfloat16).reshape(SOURCES_AT_ONCE, part, LANES)

        totals = []
        for head in range(2):
            total = quick(head, queries[head], *parts[0]) if total_ref is None else total_ref[index, head]
            totals.append(total + quick(head, queries[head], *parts[1]))
        store(totals)
        sums = jnp.concatenate([t[DH : DH + 8] for t in totals], axis=0)
        safe = jnp.logical_and(sums >= SUM_LOW, sums <= SUM_HIGH)
        unsafe = jnp.max(jnp.where(safe, 0.0, 1.0)) > 0.0

        @pl.when(unsafe)
        def _():
            if fetch_first is not None:
                fetch_first()
            pick = lax.broadcasted_iota(jnp.int32, (16, block_rows), 0) == 0
            pick = jnp.where(pick, 1.0, 0.0).astype(jnp.bfloat16)
            totals = []
            for head in range(2):

                def found(key_ref, value_ref, start, head=head):
                    live = lax.dot_general(
                        value_ref[head, DH:, pl.ds(start, SLOW_KEYS)],
                        pick,
                        CONTRACT_FIRST,
                        preferred_element_type=jnp.float32,
                    )
                    return jnp.where(live > 0.5, scores(key_ref, queries[head], start, SLOW_KEYS), -jnp.inf)

                top = jnp.full((1, block_rows), -jnp.inf, jnp.float32)
                total = jnp.zeros((DH + 16, block_rows), jnp.float32)
                for key_ref, value_ref in parts:

                    def first(i, top, key_ref=key_ref, value_ref=value_ref):
                        start = pl.multiple_of(i * SLOW_KEYS, SLOW_KEYS)
                        return jnp.maximum(top, jnp.max(found(key_ref, value_ref, start), axis=0, keepdims=True))

                    top = lax.fori_loop(0, key_ref.shape[0] // SLOW_KEYS, first, top)
                for key_ref, value_ref in parts:

                    def second(i, total, key_ref=key_ref, value_ref=value_ref, head=head, top=top):
                        start = pl.multiple_of(i * SLOW_KEYS, SLOW_KEYS)
                        weights = jnp.exp2((found(key_ref, value_ref, start) - top) * EXP2_SCALE)
                        return total + weigh(value_ref, head, weights, start, SLOW_KEYS)

                    total = lax.fori_loop(0, key_ref.shape[0] // SLOW_KEYS, second, total)
                totals.append(total)
            store(totals)

        return carry

    lax.fori_loop(0, out_ref.shape[0] // SOURCES_AT_ONCE, block, 0)


def begin_kernel(shape, part, length_ref, arrived, total_ref, keys_out, values_out, *scratch):
    rows, offset, stride = shape
    block, key_ref, value_ref, sems, out_sems = scratch
    prepare(length_ref[0], rows, offset, stride, block, arrive(arrived, block, sems, rows), key_ref, value_ref)
    kept = [
        pltpu.make_async_copy(key_ref, keys_out, out_sems.at[0]),
        pltpu.make_async_copy(value_ref, values_out, out_sems.at[1]),
    ]
    for copy in kept:
        copy.start()
    begin_rows(2 * rows, part, block, key_ref, value_ref, total_ref)
    for copy in kept:
        copy.wait()


def finish_first_kernel(shape, begin, part, length_ref, arrived, queries, *refs):
    rows, offset, stride = shape
    early_keys, early_values, total, out_ref, keys_out, values_out = refs[:6]
    block, query_block, key_ref, value_ref, early_key_ref, early_value_ref, total_ref = refs[6:13]
    sems, out_sems = refs[13:]
    arrivals = arrive(arrived, block, sems, rows)
    fetches = [
        pltpu.make_async_copy(queries.at[:, pl.ds(begin, part), :], query_block, out_sems.at[2]),
        pltpu.make_async_copy(total, total_ref, out_sems.at[3]),
    ]
    for fetch in fetches:
        fetch.start()
    prepare(length_ref[0], rows, offset, stride, block, arrivals, key_ref, value_ref)
    kept = [
        pltpu.make_async_copy(key_ref, keys_out, out_sems.at[0]),
        pltpu.make_async_copy(value_ref, values_out, out_sems.at[1]),
    ]
    for copy in kept:
        copy.start()
    for fetch in fetches:
        fetch.wait()

    def fetch_first():
        copies = [
            pltpu.make_async_copy(early_keys, early_key_ref, out_sems.at[4]),
            pltpu.make_async_copy(early_values, early_value_ref, out_sems.at[5]),
        ]
        for copy in copies:
            copy.start()
        for copy in copies:
            copy.wait()

    parts = [(early_key_ref, early_value_ref), (key_ref, value_ref)]
    finish_rows(0, part, query_block, parts, total_ref, out_ref, fetch_first)
    for copy in kept:
        copy.wait()


def finish_second_kernel(begin, part, queries, early_keys, early_values, keys, values, out_ref, query_block, sem):
    fetch = pltpu.make_async_copy(queries.at[:, pl.ds(begin, part), :], query_block, sem)
    fetch.start()
    fetch.wait()
    finish_rows(0, part, query_block, [(early_keys, early_values), (keys, values)], None, out_ref)


def call(kernel, in_specs, out_specs, out_shape, args, work, scratch):
    return pl.pallas_call(
        kernel,
        in_specs=in_specs,
        out_specs=out_specs,
        out_shape=out_shape,
        scratch_shapes=scratch,
        compiler_params=pltpu.CompilerParams(vmem_limit_bytes=VMEM_BYTES),
        cost_estimate=pl.CostEstimate(flops=work * 2 * 512 * 2, bytes_accessed=8 << 20, transcendentals=work * 2),
    )(*args)


def bf16(*shape):
    return jax.ShapeDtypeStruct(shape, jnp.bfloat16)


def attend(valid_len, first, second, rows_first, rows_second):
    sources = first.shape[0]
    stride = rows_first + rows_second
    begins = 2 * rows_first, 2 * rows_second
    parts = first.shape[1] - begins[0], second.shape[1] - begins[1]
    groups = sources // SOURCES_AT_ONCE

    def kept(rows):
        shapes = [bf16(sources * rows, LANES), bf16(2, DH + 16, sources * rows)]
        scratch = [pltpu.VMEM(x.shape, x.dtype) for x in shapes]
        return shapes, scratch, pltpu.SemaphoreType.DMA((sources // at_once(rows),))

    def work(part, rows):
        return sources * part * sources * rows

    shapes, early_scratch, arrivals = kept(rows_first)
    total, *early = call(
        functools.partial(begin_kernel, (rows_first, 0, stride), parts[0]),
        [SMEM, HBM],
        [VMEM, HBM, HBM],
        [jax.ShapeDtypeStruct((groups, 2, DH + 16, SOURCES_AT_ONCE * parts[0]), jnp.float32)] + shapes,
        (valid_len, first),
        work(parts[0], rows_first),
        [pltpu.VMEM(first.shape, first.dtype), *early_scratch, arrivals, pltpu.SemaphoreType.DMA((2,))],
    )
    query_blocks = [pltpu.VMEM((sources, part, LANES), jnp.bfloat16) for part in parts]
    shapes, scratch, arrivals = kept(rows_second)
    mixed, *late = call(
        functools.partial(finish_first_kernel, (rows_second, rows_first, stride), begins[0], parts[0]),
        [SMEM] + [HBM] * 5,
        [VMEM, HBM, HBM],
        [bf16(sources, parts[0], LANES)] + shapes,
        (valid_len, second, first, *early, total),
        work(parts[0], rows_second),
        [
            pltpu.VMEM(second.shape, second.dtype),
            query_blocks[0],
            *scratch,
            *early_scratch,
            pltpu.VMEM(total.shape, total.dtype),
            arrivals,
            pltpu.SemaphoreType.DMA((6,)),
        ],
    )
    yield mixed
    yield call(
        functools.partial(finish_second_kernel, begins[1], parts[1]),
        [HBM] + [VMEM] * 4,
        VMEM,
        bf16(sources, parts[1], LANES),
        (second, *early, *late),
        work(parts[1], stride),
        [query_blocks[1], pltpu.SemaphoreType.DMA],
    )


def by_owner(rows):
    return rows.reshape(rows.shape[0], -1, LANES).transpose(1, 0, 2)


def by_row(blocks):
    return blocks.transpose(1, 0, 2).reshape(blocks.shape[1], -1)


def exchange(blocks):
    return lax.all_to_all(blocks, "seq", split_axis=0, concat_axis=0, tiled=True)


def on_device(enc_query, enc_key, enc_value, dec_query, enc_length, tgt_length):
    rows_local = dec_query.shape[0]
    rows = enc_key.shape[0]
    cut, query_cut = rows - rows_local, 2 * rows_local
    first = [enc_key[:cut], enc_value[:cut], dec_query, enc_query[:query_cut]]
    first = exchange(by_owner(jnp.concatenate(first, axis=0)))
    second = [enc_key[cut:], enc_value[cut:], enc_query[query_cut:]]
    second, first = lax.optimization_barrier((by_owner(jnp.concatenate(second, axis=0)), first))
    second = exchange(second)
    returned = []
    for mixed in attend(enc_length, first, second, cut, rows - cut):
        if returned:
            mixed, returned[-1] = lax.optimization_barrier((mixed, returned[-1]))
        returned.append(exchange(mixed))
    returned_cross, returned[0] = returned[0][:, :rows_local], returned[0][:, rows_local:]
    enc_mixed = jnp.concatenate([by_row(r) for r in returned], axis=0)
    first_row = lax.axis_index("seq") * rows_local
    keep_rows = first_row + jnp.arange(rows_local, dtype=jnp.int32) < tgt_length[0]
    crossed = by_row(returned_cross)
    cross_mixed = jnp.where(keep_rows[:, None], crossed, jnp.zeros_like(crossed))
    return (enc_mixed, cross_mixed)


def solution(mesh):
    return jax.shard_map(
        on_device,
        mesh=mesh,
        in_specs=(
            P(("dp", "seq"), None),
            P(("dp", "seq"), None),
            P(("dp", "seq"), None),
            P(("dp", "seq"), None),
            P("dp"),
            P("dp"),
        ),
        out_specs=(P(("dp", "seq"), None), P(("dp", "seq"), None)),
        check_vma=False,
    )
```

```python
import functools
import math

import jax
import jax.numpy as jnp
from jax import lax
from jax.experimental import pallas as pl
from jax.experimental.pallas import tpu as pltpu
from jax.sharding import PartitionSpec as P

DH = 64
LANES = 128
SCALE = 0.125
EXP2_SCALE = SCALE * math.log2(math.e)
SUM_LOW, SUM_HIGH = 2.0**-60, 2.0**100
SOURCES_AT_ONCE = 8
SLOW_KEYS = 512
VMEM_BYTES = 56 << 20
SMEM = pl.BlockSpec(memory_space=pltpu.SMEM)
VMEM = pl.BlockSpec(memory_space=pltpu.VMEM)
HBM = pl.BlockSpec(memory_space=pl.ANY)
CONTRACT_FIRST = (((0,), (0,)), ((), ()))
CONTRACT_LAST = (((1,), (1,)), ((), ()))


def prepare(length, rows, offset, stride, block_ref, copies, key_ref, value_ref):
    group = block_ref.shape[0] // len(copies)
    count = group * rows
    for g, copy in enumerate(copies):
        copy.wait()
        sources = slice(g * group, (g + 1) * group)
        keys = block_ref[sources, :rows, :].reshape(count, LANES)
        values = block_ref[sources, rows : 2 * rows, :].reshape(count, LANES)

        def live(axis, shape):
            i = lax.broadcasted_iota(jnp.int32, shape, axis)
            return i + lax.div(i, rows) * (stride - rows) + (g * group * stride + offset) < length

        here = slice(g * count, (g + 1) * count)
        kept = live(0, (count, LANES))
        zeros = jnp.zeros_like(keys)
        key_ref[here, :] = jnp.where(kept, keys, zeros)
        flipped = jnp.where(kept, values, zeros).T
        ones = jnp.where(live(1, (16, count)), 1.0, 0.0).astype(jnp.bfloat16)
        for head in range(2):
            value_ref[head, :DH, here] = flipped[head * DH : (head + 1) * DH]
            value_ref[head, DH:, here] = ones


def at_once(rows):
    return 512 // rows if 512 % rows == 0 else 4


def arrive(source, block, sems, rows):
    group = at_once(rows)
    copies = []
    for g in range(block.shape[0] // group):
        here = pl.ds(g * group, group)
        source_rows = pl.ds(0, block.shape[1])
        copies.append(pltpu.make_async_copy(source.at[here, source_rows, :], block.at[here], sems.at[g]))
        copies[-1].start()
    return copies


def scores(key_ref, queries, start, count):
    return lax.dot_general(
        key_ref[pl.ds(start, count), :], queries, CONTRACT_LAST, preferred_element_type=jnp.float32
    )


def weigh(value_ref, head, weights, start, count):
    return jnp.dot(
        value_ref[head, :, pl.ds(start, count)], weights.astype(jnp.bfloat16), preferred_element_type=jnp.float32
    )


def quick(head, queries, key_ref, value_ref):
    keys = key_ref.shape[0]
    weights = jnp.exp2(scores(key_ref, queries, 0, keys) * EXP2_SCALE)
    return weigh(value_ref, head, weights, 0, keys)


def head_queries(query_ref, sources, begin, part):
    block_rows = SOURCES_AT_ONCE * part
    queries = query_ref[sources, begin : begin + part, :].reshape(block_rows, LANES)
    lane = lax.broadcasted_iota(jnp.int32, (block_rows, LANES), 1)
    zeros = jnp.zeros_like(queries)
    return [jnp.where(lane < DH, queries, zeros), jnp.where(lane < DH, zeros, queries)]


def begin_rows(begin, part, query_ref, key_ref, value_ref, total_ref):
    def block(index, carry):
        queries = head_queries(query_ref, pl.ds(index * SOURCES_AT_ONCE, SOURCES_AT_ONCE), begin, part)
        for head in range(2):
            total_ref[index, head] = quick(head, queries[head], key_ref, value_ref)
        return carry

    lax.fori_loop(0, total_ref.shape[0], block, 0, unroll=4)


def finish_rows(begin, part, query_ref, parts, total_ref, out_ref, fetch_first=None):
    block_rows = SOURCES_AT_ONCE * part
    blocks = out_ref.shape[0] // SOURCES_AT_ONCE

    def at(index):
        sources = pl.ds(index * SOURCES_AT_ONCE, SOURCES_AT_ONCE)

        def store(totals):
            mixed = jnp.concatenate([t[:DH] / t[DH : DH + 1] for t in totals], axis=0)
            out_ref[sources] = mixed.T.astype(jnp.bfloat16).reshape(SOURCES_AT_ONCE, part, LANES)

        return head_queries(query_ref, sources, begin, part), store

    def quick_block(index, unsafe):
        queries, store = at(index)
        totals = []
        for head in range(2):
            total = quick(head, queries[head], *parts[0]) if total_ref is None else total_ref[index, head]
            totals.append(total + quick(head, queries[head], *parts[1]))
        store(totals)
        for total in totals:
            sums = total[DH : DH + 8]
            safe = jnp.logical_and(sums >= SUM_LOW, sums <= SUM_HIGH)
            unsafe = jnp.maximum(unsafe, jnp.where(safe, 0.0, 1.0))
        return unsafe

    unsafe = lax.fori_loop(0, blocks, quick_block, jnp.zeros((8, block_rows), jnp.float32), unroll=4)

    def careful_block(index, carry):
        queries, store = at(index)
        pick = lax.broadcasted_iota(jnp.int32, (16, block_rows), 0) == 0
        pick = jnp.where(pick, 1.0, 0.0).astype(jnp.bfloat16)
        totals = []
        for head in range(2):

            def found(key_ref, value_ref, start, head=head):
                live = lax.dot_general(
                    value_ref[head, DH:, pl.ds(start, SLOW_KEYS)],
                    pick,
                    CONTRACT_FIRST,
                    preferred_element_type=jnp.float32,
                )
                return jnp.where(live > 0.5, scores(key_ref, queries[head], start, SLOW_KEYS), -jnp.inf)

            top = jnp.full((1, block_rows), -jnp.inf, jnp.float32)
            total = jnp.zeros((DH + 16, block_rows), jnp.float32)
            for key_ref, value_ref in parts:

                def first(i, top, key_ref=key_ref, value_ref=value_ref):
                    start = pl.multiple_of(i * SLOW_KEYS, SLOW_KEYS)
                    return jnp.maximum(top, jnp.max(found(key_ref, value_ref, start), axis=0, keepdims=True))

                top = lax.fori_loop(0, key_ref.shape[0] // SLOW_KEYS, first, top)
            for key_ref, value_ref in parts:

                def second(i, total, key_ref=key_ref, value_ref=value_ref, head=head, top=top):
                    start = pl.multiple_of(i * SLOW_KEYS, SLOW_KEYS)
                    weights = jnp.exp2((found(key_ref, value_ref, start) - top) * EXP2_SCALE)
                    return total + weigh(value_ref, head, weights, start, SLOW_KEYS)

                total = lax.fori_loop(0, key_ref.shape[0] // SLOW_KEYS, second, total)
            totals.append(total)
        store(totals)
        return carry

    @pl.when(jnp.max(unsafe) > 0.0)
    def _():
        if fetch_first is not None:
            fetch_first()
        lax.fori_loop(0, blocks, careful_block, 0)


def begin_kernel(shape, part, length_ref, arrived, total_ref, keys_out, values_out, *scratch):
    rows, offset, stride = shape
    block, key_ref, value_ref, sems, out_sems = scratch
    prepare(length_ref[0], rows, offset, stride, block, arrive(arrived, block, sems, rows), key_ref, value_ref)
    kept = [
        pltpu.make_async_copy(key_ref, keys_out, out_sems.at[0]),
        pltpu.make_async_copy(value_ref, values_out, out_sems.at[1]),
    ]
    for copy in kept:
        copy.start()
    begin_rows(2 * rows, part, block, key_ref, value_ref, total_ref)
    for copy in kept:
        copy.wait()


def finish_first_kernel(shape, begin, part, length_ref, arrived, queries, *refs):
    rows, offset, stride = shape
    early_keys, early_values, total, out_ref, keys_out, values_out = refs[:6]
    block, query_block, key_ref, value_ref, early_key_ref, early_value_ref, total_ref = refs[6:13]
    sems, out_sems = refs[13:]
    arrivals = arrive(arrived, block, sems, rows)
    fetches = [
        pltpu.make_async_copy(queries.at[:, pl.ds(begin, part), :], query_block, out_sems.at[2]),
        pltpu.make_async_copy(total, total_ref, out_sems.at[3]),
    ]
    for fetch in fetches:
        fetch.start()
    prepare(length_ref[0], rows, offset, stride, block, arrivals, key_ref, value_ref)
    kept = [
        pltpu.make_async_copy(key_ref, keys_out, out_sems.at[0]),
        pltpu.make_async_copy(value_ref, values_out, out_sems.at[1]),
    ]
    for copy in kept:
        copy.start()
    for fetch in fetches:
        fetch.wait()

    def fetch_first():
        copies = [
            pltpu.make_async_copy(early_keys, early_key_ref, out_sems.at[4]),
            pltpu.make_async_copy(early_values, early_value_ref, out_sems.at[5]),
        ]
        for copy in copies:
            copy.start()
        for copy in copies:
            copy.wait()

    parts = [(early_key_ref, early_value_ref), (key_ref, value_ref)]
    finish_rows(0, part, query_block, parts, total_ref, out_ref, fetch_first)
    for copy in kept:
        copy.wait()


def finish_second_kernel(begin, part, queries, early_keys, early_values, keys, values, out_ref, query_block, sem):
    fetch = pltpu.make_async_copy(queries.at[:, pl.ds(begin, part), :], query_block, sem)
    fetch.start()
    fetch.wait()
    finish_rows(0, part, query_block, [(early_keys, early_values), (keys, values)], None, out_ref)


def call(kernel, in_specs, out_specs, out_shape, args, work, scratch):
    return pl.pallas_call(
        kernel,
        in_specs=in_specs,
        out_specs=out_specs,
        out_shape=out_shape,
        scratch_shapes=scratch,
        compiler_params=pltpu.CompilerParams(vmem_limit_bytes=VMEM_BYTES),
        cost_estimate=pl.CostEstimate(flops=work * 2 * 512 * 2, bytes_accessed=8 << 20, transcendentals=work * 2),
    )(*args)


def bf16(*shape):
    return jax.ShapeDtypeStruct(shape, jnp.bfloat16)


def attend(valid_len, first, second, rows_first, rows_second):
    sources = first.shape[0]
    stride = rows_first + rows_second
    begins = 2 * rows_first, 2 * rows_second
    parts = first.shape[1] - begins[0], second.shape[1] - begins[1]
    groups = sources // SOURCES_AT_ONCE

    def kept(rows):
        shapes = [bf16(sources * rows, LANES), bf16(2, DH + 16, sources * rows)]
        scratch = [pltpu.VMEM(x.shape, x.dtype) for x in shapes]
        return shapes, scratch, pltpu.SemaphoreType.DMA((sources // at_once(rows),))

    def work(part, rows):
        return sources * part * sources * rows

    shapes, early_scratch, arrivals = kept(rows_first)
    total, *early = call(
        functools.partial(begin_kernel, (rows_first, 0, stride), parts[0]),
        [SMEM, HBM],
        [VMEM, HBM, HBM],
        [jax.ShapeDtypeStruct((groups, 2, DH + 16, SOURCES_AT_ONCE * parts[0]), jnp.float32)] + shapes,
        (valid_len, first),
        work(parts[0], rows_first),
        [pltpu.VMEM(first.shape, first.dtype), *early_scratch, arrivals, pltpu.SemaphoreType.DMA((2,))],
    )
    query_blocks = [pltpu.VMEM((sources, part, LANES), jnp.bfloat16) for part in parts]
    shapes, scratch, arrivals = kept(rows_second)
    mixed, *late = call(
        functools.partial(finish_first_kernel, (rows_second, rows_first, stride), begins[0], parts[0]),
        [SMEM] + [HBM] * 5,
        [VMEM, HBM, HBM],
        [bf16(sources, parts[0], LANES)] + shapes,
        (valid_len, second, first, *early, total),
        work(parts[0], rows_second),
        [
            pltpu.VMEM((sources, begins[1], LANES), second.dtype),
            query_blocks[0],
            *scratch,
            *early_scratch,
            pltpu.VMEM(total.shape, total.dtype),
            arrivals,
            pltpu.SemaphoreType.DMA((6,)),
        ],
    )
    yield mixed
    yield call(
        functools.partial(finish_second_kernel, begins[1], parts[1]),
        [HBM] + [VMEM] * 4,
        VMEM,
        bf16(sources, parts[1], LANES),
        (second, *early, *late),
        work(parts[1], stride),
        [query_blocks[1], pltpu.SemaphoreType.DMA],
    )


def by_owner(rows):
    return rows.reshape(rows.shape[0], -1, LANES).transpose(1, 0, 2)


def by_row(blocks):
    return blocks.transpose(1, 0, 2).reshape(blocks.shape[1], -1)


def exchange(blocks):
    return lax.all_to_all(blocks, "seq", split_axis=0, concat_axis=0, tiled=True)


def on_device(enc_query, enc_key, enc_value, dec_query, enc_length, tgt_length):
    rows_local = dec_query.shape[0]
    rows = enc_key.shape[0]
    cut, query_cut = rows - rows_local, 2 * rows_local
    first = [enc_key[:cut], enc_value[:cut], dec_query, enc_query[:query_cut]]
    first = exchange(by_owner(jnp.concatenate(first, axis=0)))
    second = [enc_key[cut:], enc_value[cut:], enc_query[query_cut:]]
    second, first = lax.optimization_barrier((by_owner(jnp.concatenate(second, axis=0)), first))
    second = exchange(second)
    returned = []
    for mixed in attend(enc_length, first, second, cut, rows - cut):
        if returned:
            mixed, returned[-1] = lax.optimization_barrier((mixed, returned[-1]))
        returned.append(exchange(mixed))
    returned_cross, returned[0] = returned[0][:, :rows_local], returned[0][:, rows_local:]
    enc_mixed = jnp.concatenate([by_row(r) for r in returned], axis=0)
    first_row = lax.axis_index("seq") * rows_local
    keep_rows = first_row + jnp.arange(rows_local, dtype=jnp.int32) < tgt_length[0]
    crossed = by_row(returned_cross)
    cross_mixed = jnp.where(keep_rows[:, None], crossed, jnp.zeros_like(crossed))
    return (enc_mixed, cross_mixed)


def solution(mesh):
    return jax.shard_map(
        on_device,
        mesh=mesh,
        in_specs=(
            P(("dp", "seq"), None),
            P(("dp", "seq"), None),
            P(("dp", "seq"), None),
            P(("dp", "seq"), None),
            P("dp"),
            P("dp"),
        ),
        out_specs=(P(("dp", "seq"), None), P(("dp", "seq"), None)),
        check_vma=False,
    )
```
